32 devices in a mesh: wide: 8 (over z, y), narrow: 4 (over x, core).
Axes of the slice: x: 2, y: 2, z: 4, core: 2. Of those that a mesh axis runs over, the one named last changes fastest.
Arguments:
- sources: bfloat16 [8192, 768], P('wide'), may hold values from -8 to 8
- targets: bfloat16 [65536, 768], P(('wide', 'narrow')), may hold values from -8 to 8
- pair_target: int32 [8, 12], replicated, may hold values from 0 to 63, as said below
- pair_count: int32 [8], replicated, may hold values from 8 to 12
Outputs:
- source_potential: float32 [8192], P('wide')
- target_potential: float32 [65536], P(('wide', 'narrow'))
- mapped: bfloat16 [8192, 768], P('wide')
The draws below stay inside these ranges and needn't reach their ends.
Inputs may be any that keep to these rules, and one draw needn't show every extreme that they name: `pair_target`: source block s lies in row group w = s. Its slots k < 8 hold w * 8 + k, so every target block is paired with some source block. Its other 4 slots hold distinct target blocks of groups w - 1 and w + 1 (taken modulo the number of groups); slot 8 + m holds a block whose position within its group, divided by 2 and rounded down, equals m modulo (4).
All inputs are finite; a program needn't handle non-finite values.
Results may differ from the reference program's by a relative error of at most 0.0044.
Values may be sent and summed in bfloat16 or wider, within the bound.
A program may use at most 192 MiB of HBM per device.

```python
import math
import jax
import jax.numpy as jnp
from jax import lax

D = 768
BLK = 1024
TB_DEV = 2
SB_DEV = 1
EXTRA = 4
ITERS = 2
TBG = 8
COVER = 8
NSB = 8
NTB = 64
NS = 8192
NT = 65536


def target_values(key, row_ids):
    base_key = jax.random.fold_in(key, 11)

    def draw_row(row_index):
        row_key = jax.random.fold_in(base_key, row_index)
        return jnp.clip(jax.random.normal(row_key, (D,), jnp.float32), -6.0, 6.0)
    return jax.vmap(draw_row)(row_ids)


def draw_targets(key, part):
    row_ids = jnp.arange(NT, dtype=jnp.int32)
    return target_values(key, row_ids).astype(jnp.bfloat16)


def draw_sources(key, part):
    source_key = jax.random.fold_in(key, 23)
    return jnp.clip(jax.random.normal(source_key, (NS, D), jnp.float32), -6.0, 6.0).astype(jnp.bfloat16)


def draw_pair_count(key, part):
    first_key = jax.random.fold_in(key, 31)
    second_key = jax.random.fold_in(key, 32)
    chosen_key = jax.random.fold_in(key, 33)
    extra_count = jnp.minimum(jax.random.randint(first_key, (NSB,), 0, EXTRA + 1), jax.random.randint(second_key, (NSB,), 0, EXTRA + 1))
    chosen = jax.random.randint(chosen_key, (), 0, NSB)
    block_ids = jnp.arange(NSB, dtype=jnp.int32)
    counts = COVER + extra_count
    counts = jnp.where(block_ids == chosen, COVER + EXTRA, counts)
    counts = jnp.where(block_ids == (chosen + 1) % NSB, COVER, counts)
    return counts.astype(jnp.int32)


def draw_pair_target(key, part):
    block_ids = jnp.arange(NSB, dtype=jnp.int32)
    group_ids = block_ids // SB_DEV
    within = block_ids % SB_DEV
    cover_ids = group_ids[:, None] * TBG + within[:, None] * COVER + jnp.arange(COVER, dtype=jnp.int32)[None, :]
    columns = TBG // TB_DEV
    choices_count = 2 * TB_DEV
    scores = jax.random.randint(jax.random.fold_in(key, 41), (NSB, columns, choices_count), 0, 1 << 20) * choices_count + jnp.arange(choices_count, dtype=jnp.int32)[None, None, :]
    order = jnp.argsort(scores, axis=2).astype(jnp.int32)
    slot_ids = jnp.arange(EXTRA, dtype=jnp.int32)
    slot_column = slot_ids % columns
    slot_rank = slot_ids // columns
    picked = order[:, slot_column, slot_rank]
    group_count = NSB // SB_DEV
    side_shift = jnp.where(picked < TB_DEV, -1, 1)
    owner_group = (group_ids[:, None] + side_shift + group_count) % group_count
    extra_ids = owner_group * TBG + slot_column[None, :] * TB_DEV + picked % TB_DEV
    return jnp.concatenate([cover_ids, extra_ids], axis=1).astype(jnp.int32)


def setup_inputs(seed: int = 0) -> dict:
    keys = jax.random.split(jax.random.key(seed), 5)
    sources = draw_sources(jax.random.fold_in(keys[4], 71), 0)
    targets = draw_targets(jax.random.fold_in(keys[4], 71), 0)
    pair_target = draw_pair_target(jax.random.fold_in(keys[4], 71), 0)
    pair_count = draw_pair_count(jax.random.fold_in(keys[4], 71), 0)
    return dict(sources=sources, targets=targets, pair_target=pair_target, pair_count=pair_count)


epsilon = 0.25
sentinel = -1e+30

def block_products(sources, targets, pair_target):
    source_view = sources.reshape(NSB, BLK, D)
    target_view = targets.reshape(NTB, BLK, D)

    def per_block(block_index):
        row_block = source_view[block_index].astype(jnp.float32)
        col_blocks = target_view[pair_target[block_index]].astype(jnp.float32)
        return jnp.einsum('rd,pcd->prc', row_block, col_blocks)
    return lax.map(per_block, jnp.arange(NSB, dtype=jnp.int32))

def row_scores(product, potential, alive):
    inv_root = 1.0 / math.sqrt(D)
    scores = (potential[:, None, :] + product * inv_root) * (1.0 / epsilon)
    return jnp.where(alive[:, None, None], scores, sentinel)

def row_lse(products, pair_target, live_slots, target_pot):
    pot_blocks = target_pot.reshape(NTB, BLK)[pair_target]

    def per_block(inputs):
        product, potential, alive = inputs
        scores = row_scores(product, potential, alive)
        highest = lax.optimization_barrier(jnp.max(scores, axis=(0, 2)))
        return highest + jnp.log(lax.optimization_barrier(jnp.sum(jnp.exp(scores - highest[None, :, None]), axis=(0, 2))))
    return lax.map(per_block, (products, pot_blocks, live_slots)).reshape(-1)

def col_lse(products, pair_target, live_slots, source_pot):
    inv_root = 1.0 / math.sqrt(D)
    source_rows = source_pot.reshape(NSB, BLK)

    def per_block(inputs):
        product, potential, alive = inputs
        scores = (potential[None, :, None] + product * inv_root) * (1.0 / epsilon)
        highest = lax.optimization_barrier(jnp.max(scores, axis=1))
        partial_value = highest + jnp.log(lax.optimization_barrier(jnp.sum(jnp.exp(scores - highest[:, None, :]), axis=1)))
        return jnp.where(alive[:, None], partial_value, sentinel)
    partials = lax.map(per_block, (products, source_rows, live_slots))
    flat = partials.reshape(-1, BLK)
    block_ids = pair_target.reshape(-1)

    def per_target(target_index):
        member = block_ids == target_index
        highest = lax.optimization_barrier(jnp.max(jnp.where(member[:, None], flat, sentinel), axis=0))
        shifted = jnp.where(member[:, None], flat - highest[None, :], sentinel)
        return highest + jnp.log(lax.optimization_barrier(jnp.sum(jnp.exp(shifted), axis=0)))
    return lax.map(per_target, jnp.arange(NTB, dtype=jnp.int32)).reshape(-1)

def reference(sources, targets, pair_target, pair_count):
    slots = pair_target.shape[1]
    live_slots = jnp.arange(slots, dtype=jnp.int32)[None, :] < pair_count[:, None]
    products = block_products(sources, targets, pair_target)
    target_pot = jnp.zeros((NT,), jnp.float32)
    for iteration in range(ITERS):
        source_pot = epsilon * (-math.log(NS) - row_lse(products, pair_target, live_slots, target_pot))
        target_pot = epsilon * (-math.log(NT) - col_lse(products, pair_target, live_slots, source_pot))
    final_lse = row_lse(products, pair_target, live_slots, target_pot)
    source_pot = epsilon * (-math.log(NS) - final_lse)
    pot_blocks = target_pot.reshape(NTB, BLK)[pair_target]
    lse_blocks = final_lse.reshape(NSB, BLK)
    target_view = targets.reshape(NTB, BLK, D)

    def per_block(inputs):
        product, potential, alive, lse_rows, block_index = inputs
        scores = row_scores(product, potential, alive)
        weights = jnp.where(alive[:, None, None], jnp.exp(scores - lse_rows[None, :, None]), 0.0)
        weights = lax.optimization_barrier(weights.astype(jnp.bfloat16)).astype(jnp.float32)
        col_blocks = target_view[pair_target[block_index]].astype(jnp.float32)
        return jnp.einsum('prc,pcd->rd', weights, col_blocks)
    numer = lax.map(per_block, (products, pot_blocks, live_slots, lse_blocks, jnp.arange(NSB, dtype=jnp.int32)))
    mapped = numer.reshape(NS, D).astype(jnp.bfloat16)
    return (source_pot, target_pot, mapped)
```

```python
import functools
import math

import jax
import jax.numpy as jnp
from jax import lax
from jax.experimental import pallas as pl
from jax.experimental.pallas import tpu as pltpu
from jax.sharding import PartitionSpec as P

BLK = 1024
ITERS = 2
CH = 256
NCH = BLK // CH
LANES = 128
ROWS = 16
HALF = BLK // 2
PIECE = 128
NPIECE = HALF // PIECE

epsilon = 0.25
dead = -1e30
LOG2E = math.log2(math.e)
LN2 = math.log(2.0)
MESH = pl.DeviceIdType.MESH


def log2(x):
    return jnp.log(x) * LOG2E


def lse2(terms):
    top = functools.reduce(jnp.maximum, terms)
    return top, [jnp.exp2(t - top) for t in terms]


def kernel(
    wide_count, narrow_count, consts,
    plan_ref, count_ref, src_ref, tgt_ref,
    fpot_ref, gpot_ref, map_ref,
    scores, ship, landed, extra, bcast, vec, own_lse,
    row_box, col_box, far_box, bvec, part_out, part_in, cross_out, cross_in,
    ship_s, ship_r, row_s, row_r, col_s, col_r, far_s, far_r,
    part_s, part_r, cross_s, cross_r, fin_s, fin_r,
):
    scale, lsrc, ltgt, group_blocks, tgt_blocks = consts
    w = lax.axis_index("wide")
    c = lax.axis_index("narrow")

    def wide_at(d):
        return lax.rem(w + d + wide_count, wide_count)

    mates = [c + 1 - 2 * lax.rem(c, 2), c + 2 - 4 * (c // 2), 3 - c]
    wide_steps = (1, -1, 2, -2)

    barrier = pltpu.get_barrier_semaphore()
    for m in mates:
        pl.semaphore_signal(barrier, inc=1, device_id=(w, m), device_id_type=MESH)
    for d in wide_steps:
        pl.semaphore_signal(barrier, inc=1, device_id=(wide_at(d), c), device_id_type=MESH)
    pl.semaphore_wait(barrier, 7)

    slot = group_blocks + c

    def extra_of(d):
        g = wide_at(d)
        block = plan_ref[g, slot]
        live = count_ref[g] > slot
        return block, live

    my_block, my_live = extra_of(0)
    my_group = my_block // group_blocks
    from_before = my_group == wide_at(-1)
    my_pos = lax.rem(my_block, tgt_blocks)
    base = w * group_blocks + c * tgt_blocks

    def as_weight(flag, shape):
        return jnp.full(shape, jnp.where(flag, 1.0, 0.0), jnp.float32).astype(jnp.bfloat16)

    def pick(flag, a, b):
        return a * as_weight(flag, a.shape) + b * as_weight(jnp.logical_not(flag), b.shape)

    def ship_copy(k, ch):
        rows = pl.ds(pl.multiple_of(ch * CH, CH), CH)
        return pltpu.make_async_remote_copy(
            src_ref=ship.at[k, rows, :], dst_ref=landed.at[k, rows, :],
            send_sem=ship_s.at[k, ch], recv_sem=ship_r.at[k, ch],
            device_id=(wide_at(wide_steps[k]), c), device_id_type=MESH,
        )

    asked = [lax.rem(extra_of(d)[0], tgt_blocks) == 0 for d in (1, -1)]

    def ship_chunk(ch, carry):
        r0 = pl.multiple_of(ch * CH, CH)
        first = tgt_ref[pl.ds(r0, CH), :]
        second = tgt_ref[pl.ds(BLK + r0, CH), :]
        for k in range(2):
            ship[k, pl.ds(r0, CH), :] = pick(asked[k], first, second)
            ship_copy(k, ch).start()
        return carry

    lax.fori_loop(0, NCH, ship_chunk, 0)

    eye = (
        lax.broadcasted_iota(jnp.int32, (LANES, LANES), 0)
        == lax.broadcasted_iota(jnp.int32, (LANES, LANES), 1)
    )

    def dots_into(t, ch, chunk):
        cols = pl.ds(pl.multiple_of(ch * CH, CH), CH)
        scores[t, :, cols] = lax.dot_general(
            src_ref[...], chunk, (((1,), (1,)), ((), ())), preferred_element_type=jnp.float32
        ) * scale

    def own_dots(i, carry):
        r0 = pl.multiple_of(i * CH, CH)
        dots_into(i // NCH, lax.rem(i, NCH), tgt_ref[pl.ds(r0, CH), :])
        return carry

    lax.fori_loop(0, 2 * NCH, own_dots, 0)

    def row_pass(tiles, shifts):
        def step(i, carry):
            rows = pl.ds(pl.multiple_of(i * ROWS, ROWS), ROWS)
            xs = [
                scores[t, rows, :] if b is None else scores[t, rows, :] + b
                for t, b in zip(tiles, shifts)
            ]
            top = functools.reduce(jnp.maximum, xs)
            top = jnp.max(top, axis=1, keepdims=True)
            total = functools.reduce(jnp.add, [jnp.exp2(x - top) for x in xs])
            total = jnp.sum(total, axis=1, keepdims=True)
            bcast[rows, :] = jnp.broadcast_to(top + log2(total), (ROWS, LANES))
            return carry

        lax.fori_loop(0, BLK // ROWS, step, 0)
        for g in range(BLK // LANES):
            part = bcast[g * LANES:(g + 1) * LANES, :]
            vec[:, g * LANES:(g + 1) * LANES] = jnp.sum(
                jnp.where(eye, part, 0.0), axis=0, keepdims=True
            )
        return vec[...]

    def spread(v):
        for g in range(BLK // LANES):
            part = jnp.broadcast_to(v[:, g * LANES:(g + 1) * LANES], (LANES, LANES))
            col = jnp.sum(jnp.where(eye, part, 0.0), axis=1, keepdims=True)
            bcast[g * LANES:(g + 1) * LANES, :] = jnp.broadcast_to(col, (LANES, LANES))

    def col_pass(t):
        groups = BLK // LANES

        def top_step(i, tops):
            rows = pl.ds(pl.multiple_of(i * 32, 32), 32)
            a = bcast[rows, :]
            out = []
            for g in range(groups):
                x = scores[t, rows, g * LANES:(g + 1) * LANES] + a
                out.append(jnp.maximum(tops[g], jnp.max(x.reshape(4, 8, LANES), axis=0)))
            return tuple(out)

        tops = lax.fori_loop(
            0, BLK // 32, top_step,
            tuple(jnp.full((8, LANES), dead, jnp.float32) for _ in range(groups)),
        )
        tops = [jnp.max(x, axis=0, keepdims=True) for x in tops]

        def sum_step(i, sums):
            rows = pl.ds(pl.multiple_of(i * 32, 32), 32)
            a = bcast[rows, :]
            out = []
            for g in range(groups):
                x = scores[t, rows, g * LANES:(g + 1) * LANES] + a
                e = jnp.exp2(x - tops[g])
                out.append(sums[g] + jnp.sum(e.reshape(4, 8, LANES), axis=0))
            return tuple(out)

        sums = lax.fori_loop(
            0, BLK // 32, sum_step,
            tuple(jnp.zeros((8, LANES), jnp.float32) for _ in range(groups)),
        )
        return jnp.concatenate(
            [m + log2(jnp.sum(s, axis=0, keepdims=True)) for m, s in zip(tops, sums)], axis=1
        )

    def row_round(it, mine):
        row_box[it, 0] = mine
        copies = []
        for j in range(3):
            copies.append(pltpu.make_async_remote_copy(
                src_ref=row_box.at[it, 0], dst_ref=row_box.at[it, j + 1],
                send_sem=row_s.at[it, j], recv_sem=row_r.at[it, j],
                device_id=(w, mates[j]), device_id_type=MESH,
            ))
            copies[-1].start()
        for cp in copies:
            cp.wait()
        top, e = lse2([row_box[it, j] for j in range(4)])
        return top + log2((e[0] + e[1]) + (e[2] + e[3]))

    def matches(d, block):
        b, live = extra_of(d)
        return jnp.logical_and(live, b == block)

    def merge(first, others):
        terms = [first] + [jnp.where(flag, x, dead) for flag, x in others]
        top, e = lse2(terms)
        return top + log2(functools.reduce(jnp.add, e))

    def col_round(it):
        for t in range(3):
            col_box[it, 0, t] = col_pass(t)
        copies = []
        for k in range(2):
            copies.append(pltpu.make_async_remote_copy(
                src_ref=col_box.at[it, 0], dst_ref=col_box.at[it, k + 1],
                send_sem=col_s.at[it, k], recv_sem=col_r.at[it, k],
                device_id=(wide_at(wide_steps[k]), c), device_id_type=MESH,
            ))
        for k in range(2):
            copies.append(pltpu.make_async_remote_copy(
                src_ref=col_box.at[it, 0, 2], dst_ref=far_box.at[it, k],
                send_sem=far_s.at[it, k], recv_sem=far_r.at[it, k],
                device_id=(wide_at(wide_steps[k + 2]), c), device_id_type=MESH,
            ))
        for cp in copies:
            cp.start()
        for cp in copies:
            cp.wait()
        before, after = col_box[it, 1, 2], col_box[it, 2, 2]
        for b in range(2):
            total = merge(
                col_box[it, 0, b],
                [(matches(-1, base + b), before), (matches(1, base + b), after)],
            )
            bvec[b] = ltgt - total
        owner = jnp.where(
            from_before,
            jnp.where(my_pos == 0, col_box[it, 1, 0], col_box[it, 1, 1]),
            jnp.where(my_pos == 0, col_box[it, 2, 0], col_box[it, 2, 1]),
        )
        third_flag = jnp.where(
            from_before,
            jnp.where(matches(-2, my_block), 1, 0),
            jnp.where(matches(2, my_block), 1, 0),
        ) == 1
        third = jnp.where(from_before, far_box[it, 0], far_box[it, 1])
        total = merge(owner, [(my_live, col_box[it, 0, 2]), (third_flag, third)])
        bvec[2] = jnp.where(my_live, ltgt - total, dead)

    own_lse[...] = row_pass([0, 1], [None, None])

    def land(ch, carry):
        rows = pl.ds(pl.multiple_of(ch * CH, CH), CH)
        for k in range(2):
            ship_copy(k, ch).wait()
        chunk = pick(from_before, landed[0, rows, :], landed[1, rows, :])
        extra[rows, :] = chunk
        dots_into(2, ch, chunk)
        return carry

    lax.fori_loop(0, NCH, land, 0)

    extra_lse = jnp.where(my_live, row_pass([2], [None]), dead)
    top, e = lse2([own_lse[...], extra_lse])
    total = row_round(0, top + log2(e[0] + e[1]))
    for it in range(ITERS):
        spread(lsrc - total)
        col_round(it)
        total = row_round(it + 1, row_pass([0, 1, 2], [bvec[0], bvec[1], bvec[2]]))
    fpot_ref[...] = (epsilon * LN2) * (lsrc - total)
    for b in range(2):
        gpot_ref[b] = (epsilon * LN2) * bvec[b]
    spread(total)

    def bary(r0):
        rows = pl.ds(pl.multiple_of(r0, PIECE), PIECE)
        level = bcast[rows, :]
        level = jnp.concatenate([level] * (BLK // LANES), axis=1)
        numer = None
        for t in range(3):
            weights = jnp.exp2(scores[t, rows, :] + bvec[t] - level).astype(jnp.bfloat16)
            block = extra[...] if t == 2 else tgt_ref[t * BLK:(t + 1) * BLK, :]
            term = jnp.dot(weights, block, preferred_element_type=jnp.float32)
            numer = term if numer is None else numer + term
        return numer

    side = lax.rem(c, 2)
    mine0 = side * HALF
    theirs0 = HALF - mine0

    def piece_rows(p):
        return pl.ds(pl.multiple_of(p * PIECE, PIECE), PIECE)

    def part_copy(p):
        return pltpu.make_async_remote_copy(
            src_ref=part_out.at[piece_rows(p), :], dst_ref=part_in.at[piece_rows(p), :],
            send_sem=part_s.at[p], recv_sem=part_r.at[p],
            device_id=(w, mates[0]), device_id_type=MESH,
        )

    def cross_copy(p):
        return pltpu.make_async_remote_copy(
            src_ref=cross_out.at[piece_rows(p), :], dst_ref=cross_in.at[piece_rows(p), :],
            send_sem=cross_s.at[p], recv_sem=cross_r.at[p],
            device_id=(w, mates[1]), device_id_type=MESH,
        )

    def final_copy(p):
        rows = pl.ds(pl.multiple_of(mine0 + p * PIECE, PIECE), PIECE)
        return pltpu.make_async_remote_copy(
            src_ref=map_ref.at[rows, :], dst_ref=map_ref.at[rows, :],
            send_sem=fin_s.at[p], recv_sem=fin_r.at[p],
            device_id=(w, mates[0]), device_id_type=MESH,
        )

    def send_part(p, carry):
        part_out[piece_rows(p), :] = bary(theirs0 + p * PIECE).astype(jnp.bfloat16)
        part_copy(p).start()
        mine = bary(mine0 + p * PIECE)
        part_copy(p).wait()
        mine = mine + part_in[piece_rows(p), :].astype(jnp.float32)
        cross_out[piece_rows(p), :] = mine.astype(jnp.bfloat16)
        cross_copy(p).start()
        return carry

    lax.fori_loop(0, NPIECE, send_part, 0)

    def finish(p, carry):
        cross_copy(p).wait()
        both = cross_out[piece_rows(p), :].astype(jnp.float32) + cross_in[
            piece_rows(p), :
        ].astype(jnp.float32)
        rows = pl.ds(pl.multiple_of(mine0 + p * PIECE, PIECE), PIECE)
        map_ref[rows, :] = both.astype(jnp.bfloat16)
        final_copy(p).start()
        return carry

    lax.fori_loop(0, NPIECE, finish, 0)

    def drain(p, carry):
        final_copy(p).wait()
        return carry

    lax.fori_loop(0, NPIECE, drain, 0)


def shards(sources, targets, pair_target, pair_count):
    features = sources.shape[1]
    src_blocks = sources.shape[0] // BLK
    tgt_blocks = targets.shape[0] // BLK
    wide_count = lax.axis_size("wide")
    narrow_count = lax.axis_size("narrow")
    group_blocks = tgt_blocks * narrow_count
    assert src_blocks == 1 and tgt_blocks == 2 and narrow_count == 4
    assert pair_target.shape[1] == group_blocks + narrow_count and wide_count >= 5
    scale = LOG2E / (math.sqrt(features) * epsilon)
    lsrc = -math.log2(wide_count * src_blocks * BLK)
    ltgt = -math.log2(wide_count * narrow_count * tgt_blocks * BLK)
    consts = (scale, lsrc, ltgt, group_blocks, tgt_blocks)
    vm = pl.BlockSpec(memory_space=pltpu.VMEM)
    sm = pl.BlockSpec(memory_space=pltpu.SMEM)
    f32, bf16 = jnp.float32, jnp.bfloat16
    rounds = ITERS + 1
    dma = pltpu.SemaphoreType.DMA
    fpot, gpot, mapped = pl.pallas_call(
        functools.partial(kernel, wide_count, narrow_count, consts),
        out_shape=(
            jax.ShapeDtypeStruct((1, BLK), f32),
            jax.ShapeDtypeStruct((tgt_blocks, 1, BLK), f32),
            jax.ShapeDtypeStruct((BLK, features), bf16),
        ),
        in_specs=[sm, sm, vm, vm],
        out_specs=(vm, vm, vm),
        scratch_shapes=[
            pltpu.VMEM((3, BLK, BLK), f32),
            pltpu.VMEM((2, BLK, features), bf16),
            pltpu.VMEM((2, BLK, features), bf16),
            pltpu.VMEM((BLK, features), bf16),
            pltpu.VMEM((BLK, LANES), f32),
            pltpu.VMEM((1, BLK), f32),
            pltpu.VMEM((1, BLK), f32),
            pltpu.VMEM((rounds, 4, 1, BLK), f32),
            pltpu.VMEM((ITERS, 3, 3, 1, BLK), f32),
            pltpu.VMEM((ITERS, 2, 1, BLK), f32),
            pltpu.VMEM((3, 1, BLK), f32),
            pltpu.VMEM((HALF, features), bf16),
            pltpu.VMEM((HALF, features), bf16),
            pltpu.VMEM((HALF, features), bf16),
            pltpu.VMEM((HALF, features), bf16),
            dma((2, NCH)), dma((2, NCH)),
            dma((rounds, 3)), dma((rounds, 3)),
            dma((ITERS, 2)), dma((ITERS, 2)),
            dma((ITERS, 2)), dma((ITERS, 2)),
            dma((NPIECE,)), dma((NPIECE,)),
            dma((NPIECE,)), dma((NPIECE,)),
            dma((NPIECE,)), dma((NPIECE,)),
        ],
        compiler_params=pltpu.CompilerParams(
            collective_id=0, has_side_effects=True, vmem_limit_bytes=48 * 1024 * 1024
        ),
        cost_estimate=pl.CostEstimate(
            flops=12 * BLK * BLK * features, bytes_accessed=8 * BLK * features,
            transcendentals=18 * BLK * BLK,
        ),
    )(pair_target, pair_count, sources, targets)
    return (fpot.reshape(-1), gpot.reshape(-1), mapped)


def solution(mesh):
    placed = (P("wide", None), P(("wide", "narrow"), None), P(), P())
    return jax.shard_map(
        shards,
        mesh=mesh,
        in_specs=placed,
        out_specs=(P("wide"), P(("wide", "narrow")), P("wide", None)),
        check_vma=False,
    )
```

```python
import functools
import math

import jax
import jax.numpy as jnp
from jax import lax
from jax.experimental import pallas as pl
from jax.experimental.pallas import tpu as pltpu
from jax.sharding import PartitionSpec as P

BLK = 1024
ITERS = 2
CH = 256
NCH = BLK // CH
SHIP = 128
NSHIP = BLK // SHIP
LANES = 128
ROWS = 16
STRIP = 64
HALF = BLK // 2
PIECE = 256
NPIECE = HALF // PIECE

epsilon = 0.25
dead = -1e30
LOG2E = math.log2(math.e)
LN2 = math.log(2.0)
MESH = pl.DeviceIdType.MESH


def log2(x):
    return jnp.log(x) * LOG2E


def lse2(terms):
    top = functools.reduce(jnp.maximum, terms)
    return top, [jnp.exp2(t - top) for t in terms]


def tree(op, terms):
    while len(terms) > 1:
        pairs = [op(a, b) for a, b in zip(terms[::2], terms[1::2])]
        terms = pairs + terms[len(terms) - len(terms) % 2:]
    return terms[0]


def kernel(
    wide_count, narrow_count, consts,
    plan_ref, count_ref, src_ref, tgt_ref,
    fpot_ref, gpot_ref, map_ref,
    scores, relay_out, relay_in, ship, extra, bcast, lane_top, lane_sum, vec, own_lse,
    row_box, col_box, far_box, bvec, part_out, part_in, cross_out, cross_in,
    relay_s, relay_r, ship_s, ship_r, row_s, row_r, col_s, col_r, far_s, far_r,
    part_s, part_r, cross_s, cross_r, fin_s, fin_r,
):
    scale, lsrc, ltgt, group_blocks, tgt_blocks = consts
    w = lax.axis_index("wide")
    c = lax.axis_index("narrow")

    def wide_at(d):
        return lax.rem(w + d + wide_count, wide_count)

    mates = [c + 1 - 2 * lax.rem(c, 2), c + 2 - 4 * (c // 2), 3 - c]
    wide_steps = (1, -1, 2, -2)

    barrier = pltpu.get_barrier_semaphore()
    for m in mates:
        pl.semaphore_signal(barrier, inc=1, device_id=(w, m), device_id_type=MESH)
    for d in wide_steps:
        pl.semaphore_signal(barrier, inc=1, device_id=(wide_at(d), c), device_id_type=MESH)
    pl.semaphore_wait(barrier, 7)

    slot = group_blocks + c

    def extra_of(d):
        g = wide_at(d)
        block = plan_ref[g, slot]
        live = count_ref[g] > slot
        return block, live

    my_block, my_live = extra_of(0)
    my_group = my_block // group_blocks
    from_before = my_group == wide_at(-1)
    my_pos = lax.rem(my_block, tgt_blocks)
    base = w * group_blocks + c * tgt_blocks

    def as_weight(flag, shape):
        return jnp.full(shape, jnp.where(flag, 1.0, 0.0), jnp.float32).astype(jnp.bfloat16)

    def pick(flag, a, b):
        return a * as_weight(flag, a.shape) + b * as_weight(jnp.logical_not(flag), b.shape)

    even = lax.rem(w, 2) == 0
    away = jnp.where(even, wide_at(-2), wide_at(2))
    partner = jnp.where(even, w + 1, w - 1)
    user = jnp.where(even, wide_at(-1), wide_at(1))

    def chunk_rows(ch):
        return pl.ds(pl.multiple_of(ch * SHIP, SHIP), SHIP)

    def relay_copy(ch):
        return pltpu.make_async_remote_copy(
            src_ref=relay_out.at[chunk_rows(ch), :], dst_ref=relay_in.at[chunk_rows(ch), :],
            send_sem=relay_s.at[ch], recv_sem=relay_r.at[ch],
            device_id=(away, c), device_id_type=MESH,
        )

    def ship_copy(ch):
        return pltpu.make_async_remote_copy(
            src_ref=ship.at[chunk_rows(ch), :], dst_ref=extra.at[chunk_rows(ch), :],
            send_sem=ship_s.at[ch], recv_sem=ship_r.at[ch],
            device_id=(partner, c), device_id_type=MESH,
        )

    def own_chunk(first_wanted, ch):
        r0 = pl.multiple_of(ch * SHIP, SHIP)
        return pick(first_wanted, tgt_ref[pl.ds(r0, SHIP), :], tgt_ref[pl.ds(BLK + r0, SHIP), :])

    user_first = lax.rem(plan_ref[user, slot], tgt_blocks) == 0
    partner_block = plan_ref[partner, slot]
    partner_first = lax.rem(partner_block, tgt_blocks) == 0
    partner_mine = partner_block // group_blocks == w

    def relay_chunk(ch, carry):
        relay_out[chunk_rows(ch), :] = own_chunk(user_first, ch)
        relay_copy(ch).start()
        return carry

    lax.fori_loop(0, NSHIP, relay_chunk, 0)

    eye = (
        lax.broadcasted_iota(jnp.int32, (LANES, LANES), 0)
        == lax.broadcasted_iota(jnp.int32, (LANES, LANES), 1)
    )

    def dots_into(t, ch, chunk):
        cols = pl.ds(pl.multiple_of(ch * CH, CH), CH)
        scores[t, :, cols] = lax.dot_general(
            src_ref[...], chunk, (((1,), (1,)), ((), ())), preferred_element_type=jnp.float32
        ) * scale

    def own_dots(i):
        r0 = pl.multiple_of(i * CH, CH)
        dots_into(i // NCH, lax.rem(i, NCH), tgt_ref[pl.ds(r0, CH), :])

    def land(i):
        ship_copy(2 * i).wait()
        ship_copy(2 * i + 1).wait()
        dots_into(2, i, extra[pl.ds(pl.multiple_of(i * CH, CH), CH), :])

    def forward(ch, carry):
        own_dots(ch)
        relay_copy(ch).wait()
        ship[chunk_rows(ch), :] = pick(
            partner_mine, own_chunk(partner_first, ch), relay_in[chunk_rows(ch), :]
        )
        ship_copy(ch).start()

        @pl.when(jnp.logical_and(lax.rem(ch, 2) == 1, ch >= 3))
        def _():
            land((ch - 3) // 2)

        return carry

    lax.fori_loop(0, NSHIP, forward, 0)

    def row_pass(tiles, shifts):
        def step(i, carry):
            for h in range(2):
                rows = pl.ds(pl.multiple_of((2 * i + h) * ROWS, ROWS), ROWS)
                xs = []
                for t, b in zip(tiles, shifts):
                    for g in range(BLK // LANES):
                        x = scores[t, rows, g * LANES:(g + 1) * LANES]
                        xs.append(x if b is None else x + b[:, g * LANES:(g + 1) * LANES])
                top = tree(jnp.maximum, xs)
                lane_top[rows, :] = top
                lane_sum[rows, :] = tree(jnp.add, [jnp.exp2(x - top) for x in xs])
            return carry

        lax.fori_loop(0, BLK // (2 * ROWS), step, 0)
        for g in range(BLK // LANES):
            rows = slice(g * LANES, (g + 1) * LANES)
            tops = lane_top[rows, :]
            top = jnp.max(tops, axis=1, keepdims=True)
            total = jnp.sum(lane_sum[rows, :] * jnp.exp2(tops - top), axis=1, keepdims=True)
            part = jnp.broadcast_to(top + log2(total), (LANES, LANES))
            vec[:, g * LANES:(g + 1) * LANES] = jnp.sum(
                jnp.where(eye, part, 0.0), axis=0, keepdims=True
            )
        return vec[...]

    def spread(v):
        for g in range(BLK // LANES):
            part = jnp.broadcast_to(v[:, g * LANES:(g + 1) * LANES], (LANES, LANES))
            col = jnp.sum(jnp.where(eye, part, 0.0), axis=1, keepdims=True)
            bcast[g * LANES:(g + 1) * LANES, :] = jnp.broadcast_to(col, (LANES, LANES))

    def col_pass(t):
        groups = BLK // LANES

        def top_step(i, tops):
            rows = pl.ds(pl.multiple_of(i * STRIP, STRIP), STRIP)
            a = bcast[rows, :]
            out = []
            for g in range(groups):
                x = scores[t, rows, g * LANES:(g + 1) * LANES] + a
                out.append(jnp.maximum(tops[g], jnp.max(x.reshape(STRIP // 8, 8, LANES), axis=0)))
            return tuple(out)

        tops = lax.fori_loop(
            0, BLK // STRIP, top_step,
            tuple(jnp.full((8, LANES), dead, jnp.float32) for _ in range(groups)),
        )
        tops = [jnp.max(x, axis=0, keepdims=True) for x in tops]

        def sum_step(i, sums):
            rows = pl.ds(pl.multiple_of(i * STRIP, STRIP), STRIP)
            a = bcast[rows, :]
            out = []
            for g in range(groups):
                x = scores[t, rows, g * LANES:(g + 1) * LANES] + a
                e = jnp.exp2(x - tops[g])
                out.append(sums[g] + jnp.sum(e.reshape(STRIP // 8, 8, LANES), axis=0))
            return tuple(out)

        sums = lax.fori_loop(
            0, BLK // STRIP, sum_step,
            tuple(jnp.zeros((8, LANES), jnp.float32) for _ in range(groups)),
        )
        return jnp.concatenate(
            [m + log2(jnp.sum(s, axis=0, keepdims=True)) for m, s in zip(tops, sums)], axis=1
        )

    def row_round(it, mine):
        row_box[it, 0] = mine
        copies = []
        for j in range(3):
            copies.append(pltpu.make_async_remote_copy(
                src_ref=row_box.at[it, 0], dst_ref=row_box.at[it, j + 1],
                send_sem=row_s.at[it, j], recv_sem=row_r.at[it, j],
                device_id=(w, mates[j]), device_id_type=MESH,
            ))
            copies[-1].start()
        for cp in copies:
            cp.wait()
        top, e = lse2([row_box[it, j] for j in range(4)])
        return top + log2((e[0] + e[1]) + (e[2] + e[3]))

    def matches(d, block):
        b, live = extra_of(d)
        return jnp.logical_and(live, b == block)

    def merge(first, others):
        terms = [first] + [jnp.where(flag, x, dead) for flag, x in others]
        top, e = lse2(terms)
        return top + log2(functools.reduce(jnp.add, e))

    def col_round(it):
        for t in range(3):
            col_box[it, 0, t] = col_pass(t)
        copies = []
        for k in range(2):
            copies.append(pltpu.make_async_remote_copy(
                src_ref=col_box.at[it, 0], dst_ref=col_box.at[it, k + 1],
                send_sem=col_s.at[it, k], recv_sem=col_r.at[it, k],
                device_id=(wide_at(wide_steps[k]), c), device_id_type=MESH,
            ))
        for k in range(2):
            copies.append(pltpu.make_async_remote_copy(
                src_ref=col_box.at[it, 0, 2], dst_ref=far_box.at[it, k],
                send_sem=far_s.at[it, k], recv_sem=far_r.at[it, k],
                device_id=(wide_at(wide_steps[k + 2]), c), device_id_type=MESH,
            ))
        for cp in copies:
            cp.start()
        for cp in copies:
            cp.wait()
        before, after = col_box[it, 1, 2], col_box[it, 2, 2]
        for b in range(2):
            total = merge(
                col_box[it, 0, b],
                [(matches(-1, base + b), before), (matches(1, base + b), after)],
            )
            bvec[b] = ltgt - total
        owner = jnp.where(
            from_before,
            jnp.where(my_pos == 0, col_box[it, 1, 0], col_box[it, 1, 1]),
            jnp.where(my_pos == 0, col_box[it, 2, 0], col_box[it, 2, 1]),
        )
        third_flag = jnp.where(
            from_before,
            jnp.where(matches(-2, my_block), 1, 0),
            jnp.where(matches(2, my_block), 1, 0),
        ) == 1
        third = jnp.where(from_before, far_box[it, 0], far_box[it, 1])
        total = merge(owner, [(my_live, col_box[it, 0, 2]), (third_flag, third)])
        bvec[2] = jnp.where(my_live, ltgt - total, dead)

    own_lse[...] = row_pass([0, 1], [None, None])

    land(NCH - 1)

    extra_lse = jnp.where(my_live, row_pass([2], [None]), dead)
    top, e = lse2([own_lse[...], extra_lse])
    total = row_round(0, top + log2(e[0] + e[1]))
    for it in range(ITERS):
        spread(lsrc - total)
        col_round(it)
        total = row_round(it + 1, row_pass([0, 1, 2], [bvec[0], bvec[1], bvec[2]]))
    fpot_ref[...] = (epsilon * LN2) * (lsrc - total)
    for b in range(2):
        gpot_ref[b] = (epsilon * LN2) * bvec[b]
    spread(total)

    def bary(r0):
        rows = pl.ds(pl.multiple_of(r0, PIECE), PIECE)
        level = bcast[rows, :]
        level = jnp.concatenate([level] * (BLK // LANES), axis=1)
        numer = None
        for t in range(3):
            weights = jnp.exp2(scores[t, rows, :] + bvec[t] - level).astype(jnp.bfloat16)
            block = extra[...] if t == 2 else tgt_ref[t * BLK:(t + 1) * BLK, :]
            term = jnp.dot(weights, block, preferred_element_type=jnp.float32)
            numer = term if numer is None else numer + term
        return numer

    side = lax.rem(c, 2)
    mine0 = side * HALF
    theirs0 = HALF - mine0

    def piece_rows(p):
        return pl.ds(pl.multiple_of(p * PIECE, PIECE), PIECE)

    def part_copy(p):
        return pltpu.make_async_remote_copy(
            src_ref=part_out.at[piece_rows(p), :], dst_ref=part_in.at[piece_rows(p), :],
            send_sem=part_s.at[p], recv_sem=part_r.at[p],
            device_id=(w, mates[0]), device_id_type=MESH,
        )

    def cross_copy(p):
        return pltpu.make_async_remote_copy(
            src_ref=cross_out.at[piece_rows(p), :], dst_ref=cross_in.at[piece_rows(p), :],
            send_sem=cross_s.at[p], recv_sem=cross_r.at[p],
            device_id=(w, mates[1]), device_id_type=MESH,
        )

    def final_copy(p):
        rows = pl.ds(pl.multiple_of(mine0 + p * PIECE, PIECE), PIECE)
        return pltpu.make_async_remote_copy(
            src_ref=map_ref.at[rows, :], dst_ref=map_ref.at[rows, :],
            send_sem=fin_s.at[p], recv_sem=fin_r.at[p],
            device_id=(w, mates[0]), device_id_type=MESH,
        )

    def send_part(p, carry):
        part_out[piece_rows(p), :] = bary(theirs0 + p * PIECE).astype(jnp.bfloat16)
        part_copy(p).start()
        mine = bary(mine0 + p * PIECE)
        part_copy(p).wait()
        mine = mine + part_in[piece_rows(p), :].astype(jnp.float32)
        cross_out[piece_rows(p), :] = mine.astype(jnp.bfloat16)
        cross_copy(p).start()
        return carry

    lax.fori_loop(0, NPIECE, send_part, 0)

    def finish(p, carry):
        cross_copy(p).wait()
        both = cross_out[piece_rows(p), :].astype(jnp.float32) + cross_in[
            piece_rows(p), :
        ].astype(jnp.float32)
        rows = pl.ds(pl.multiple_of(mine0 + p * PIECE, PIECE), PIECE)
        map_ref[rows, :] = both.astype(jnp.bfloat16)
        final_copy(p).start()
        return carry

    lax.fori_loop(0, NPIECE, finish, 0)

    def drain(p, carry):
        final_copy(p).wait()
        return carry

    lax.fori_loop(0, NPIECE, drain, 0)


def shards(sources, targets, pair_target, pair_count):
    features = sources.shape[1]
    src_blocks = sources.shape[0] // BLK
    tgt_blocks = targets.shape[0] // BLK
    wide_count = lax.axis_size("wide")
    narrow_count = lax.axis_size("narrow")
    group_blocks = tgt_blocks * narrow_count
    assert src_blocks == 1 and tgt_blocks == 2 and narrow_count == 4
    assert pair_target.shape[1] == group_blocks + narrow_count and wide_count >= 5 and wide_count % 2 == 0
    scale = LOG2E / (math.sqrt(features) * epsilon)
    lsrc = -math.log2(wide_count * src_blocks * BLK)
    ltgt = -math.log2(wide_count * narrow_count * tgt_blocks * BLK)
    consts = (scale, lsrc, ltgt, group_blocks, tgt_blocks)
    vm = pl.BlockSpec(memory_space=pltpu.VMEM)
    sm = pl.BlockSpec(memory_space=pltpu.SMEM)
    f32, bf16 = jnp.float32, jnp.bfloat16
    rounds = ITERS + 1
    dma = pltpu.SemaphoreType.DMA
    fpot, gpot, mapped = pl.pallas_call(
        functools.partial(kernel, wide_count, narrow_count, consts),
        out_shape=(
            jax.ShapeDtypeStruct((1, BLK), f32),
            jax.ShapeDtypeStruct((tgt_blocks, 1, BLK), f32),
            jax.ShapeDtypeStruct((BLK, features), bf16),
        ),
        in_specs=[sm, sm, vm, vm],
        out_specs=(vm, vm, vm),
        scratch_shapes=[
            pltpu.VMEM((3, BLK, BLK), f32),
            pltpu.VMEM((BLK, features), bf16),
            pltpu.VMEM((BLK, features), bf16),
            pltpu.VMEM((BLK, features), bf16),
            pltpu.VMEM((BLK, features), bf16),
            pltpu.VMEM((BLK, LANES), f32),
            pltpu.VMEM((BLK, LANES), f32),
            pltpu.VMEM((BLK, LANES), f32),
            pltpu.VMEM((1, BLK), f32),
            pltpu.VMEM((1, BLK), f32),
            pltpu.VMEM((rounds, 4, 1, BLK), f32),
            pltpu.VMEM((ITERS, 3, 3, 1, BLK), f32),
            pltpu.VMEM((ITERS, 2, 1, BLK), f32),
            pltpu.VMEM((3, 1, BLK), f32),
            pltpu.VMEM((HALF, features), bf16),
            pltpu.VMEM((HALF, features), bf16),
            pltpu.VMEM((HALF, features), bf16),
            pltpu.VMEM((HALF, features), bf16),
            dma((NSHIP,)), dma((NSHIP,)),
            dma((NSHIP,)), dma((NSHIP,)),
            dma((rounds, 3)), dma((rounds, 3)),
            dma((ITERS, 2)), dma((ITERS, 2)),
            dma((ITERS, 2)), dma((ITERS, 2)),
            dma((NPIECE,)), dma((NPIECE,)),
            dma((NPIECE,)), dma((NPIECE,)),
            dma((NPIECE,)), dma((NPIECE,)),
        ],
        compiler_params=pltpu.CompilerParams(
            collective_id=0, has_side_effects=True, vmem_limit_bytes=48 * 1024 * 1024
        ),
        cost_estimate=pl.CostEstimate(
            flops=12 * BLK * BLK * features, bytes_accessed=8 * BLK * features,
            transcendentals=18 * BLK * BLK,
        ),
    )(pair_target, pair_count, sources, targets)
    return (fpot.reshape(-1), gpot.reshape(-1), mapped)


def solution(mesh):
    placed = (P("wide", None), P(("wide", "narrow"), None), P(), P())
    return jax.shard_map(
        shards,
        mesh=mesh,
        in_specs=placed,
        out_specs=(P("wide"), P(("wide", "narrow")), P("wide", None)),
        check_vma=False,
    )
```

```python
import functools
import math

import jax
import jax.numpy as jnp
from jax import lax
from jax.experimental import pallas as pl
from jax.experimental.pallas import tpu as pltpu
from jax.sharding import PartitionSpec as P

BLK = 1024
ITERS = 2
CH = 256
NCH = BLK // CH
SHIP = 64
NSHIP = BLK // SHIP
PARTS = CH // SHIP
LANES = 128
ROWS = 16
STRIP = 64
HALF = BLK // 2
PIECE = 128
NPIECE = HALF // PIECE

epsilon = 0.25
dead = -1e30
LOG2E = math.log2(math.e)
LN2 = math.log(2.0)
MESH = pl.DeviceIdType.MESH


def log2(x):
    return jnp.log(x) * LOG2E


def lse2(terms):
    top = functools.reduce(jnp.maximum, terms)
    return top, [jnp.exp2(t - top) for t in terms]


def tree(op, terms):
    while len(terms) > 1:
        pairs = [op(a, b) for a, b in zip(terms[::2], terms[1::2])]
        terms = pairs + terms[len(terms) - len(terms) % 2:]
    return terms[0]


def kernel(
    wide_count, narrow_count, consts,
    plan_ref, count_ref, src_hbm, tgt_hbm,
    fpot_ref, gpot_ref, map_ref,
    src_ref, tgt_ref, scores, relay_out, relay_in, ship, extra, bcast, lane_top, lane_sum, vec, qvec, own_lse,
    row_box, col_box, far_box, bvec, part_out, part_in, cross_out, cross_in,
    relay_s, relay_r, ship_s, ship_r, row_s, row_r, col_s, col_r, far_s, far_r,
    part_s, part_r, cross_s, cross_r, fin_s, fin_r, load_sem,
):
    scale, lsrc, ltgt, group_blocks, tgt_blocks = consts
    w = lax.axis_index("wide")
    c = lax.axis_index("narrow")

    def wide_at(d):
        return lax.rem(w + d + wide_count, wide_count)

    mates = [c + 1 - 2 * lax.rem(c, 2), c + 2 - 4 * (c // 2), 3 - c]
    wide_steps = (1, -1, 2, -2)

    load_tgt = pltpu.make_async_copy(tgt_hbm, tgt_ref, load_sem.at[0])
    load_src = pltpu.make_async_copy(src_hbm, src_ref, load_sem.at[1])
    load_tgt.start()
    load_src.start()

    barrier = pltpu.get_barrier_semaphore()
    for m in mates:
        pl.semaphore_signal(barrier, inc=1, device_id=(w, m), device_id_type=MESH)
    for d in wide_steps:
        pl.semaphore_signal(barrier, inc=1, device_id=(wide_at(d), c), device_id_type=MESH)
    pl.semaphore_wait(barrier, 7)
    load_tgt.wait()

    slot = group_blocks + c

    def extra_of(d):
        g = wide_at(d)
        block = plan_ref[g, slot]
        live = count_ref[g] > slot
        return block, live

    my_block, my_live = extra_of(0)
    my_group = my_block // group_blocks
    from_before = my_group == wide_at(-1)
    my_pos = lax.rem(my_block, tgt_blocks)
    base = w * group_blocks + c * tgt_blocks

    def as_weight(flag, shape):
        return jnp.full(shape, jnp.where(flag, 1.0, 0.0), jnp.float32).astype(jnp.bfloat16)

    def pick(flag, a, b):
        return a * as_weight(flag, a.shape) + b * as_weight(jnp.logical_not(flag), b.shape)

    even = lax.rem(w, 2) == 0
    away = jnp.where(even, wide_at(-2), wide_at(2))
    partner = jnp.where(even, w + 1, w - 1)
    user = jnp.where(even, wide_at(-1), wide_at(1))

    def chunk_rows(ch):
        return pl.ds(pl.multiple_of(ch * SHIP, SHIP), SHIP)

    def relay_copy(ch):
        return pltpu.make_async_remote_copy(
            src_ref=relay_out.at[chunk_rows(ch), :], dst_ref=relay_in.at[chunk_rows(ch), :],
            send_sem=relay_s.at[ch], recv_sem=relay_r.at[ch],
            device_id=(away, c), device_id_type=MESH,
        )

    def ship_copy(ch):
        return pltpu.make_async_remote_copy(
            src_ref=ship.at[chunk_rows(ch), :], dst_ref=extra.at[chunk_rows(ch), :],
            send_sem=ship_s.at[ch], recv_sem=ship_r.at[ch],
            device_id=(partner, c), device_id_type=MESH,
        )

    def own_chunk(first_wanted, ch):
        r0 = pl.multiple_of(ch * SHIP, SHIP)
        return pick(first_wanted, tgt_ref[pl.ds(r0, SHIP), :], tgt_ref[pl.ds(BLK + r0, SHIP), :])

    user_first = lax.rem(plan_ref[user, slot], tgt_blocks) == 0
    partner_block = plan_ref[partner, slot]
    partner_first = lax.rem(partner_block, tgt_blocks) == 0
    partner_mine = partner_block // group_blocks == w

    def relay_chunk(ch, carry):
        relay_out[chunk_rows(ch), :] = own_chunk(user_first, ch)
        relay_copy(ch).start()
        return carry

    lax.fori_loop(0, NSHIP, relay_chunk, 0)

    eye = (
        lax.broadcasted_iota(jnp.int32, (LANES, LANES), 0)
        == lax.broadcasted_iota(jnp.int32, (LANES, LANES), 1)
    )

    def dots_into(t, ch, chunk):
        cols = pl.ds(pl.multiple_of(ch * CH, CH), CH)
        scores[t, :, cols] = lax.dot_general(
            src_ref[...], chunk, (((1,), (1,)), ((), ())), preferred_element_type=jnp.float32
        ) * scale

    def own_dots(i):
        r0 = pl.multiple_of(i * CH, CH)
        dots_into(i // NCH, lax.rem(i, NCH), tgt_ref[pl.ds(r0, CH), :])

    def land(i):
        for p in range(PARTS):
            ship_copy(PARTS * i + p).wait()
        dots_into(2, i, extra[pl.ds(pl.multiple_of(i * CH, CH), CH), :])

    load_src.wait()

    def forward(ch, carry):
        @pl.when(lax.rem(ch, 2) == 0)
        def _():
            own_dots(ch // 2)

        relay_copy(ch).wait()
        ship[chunk_rows(ch), :] = pick(
            partner_mine, own_chunk(partner_first, ch), relay_in[chunk_rows(ch), :]
        )
        ship_copy(ch).start()

        @pl.when(jnp.logical_and(lax.rem(ch, PARTS) == 1, ch > PARTS))
        def _():
            land((ch - PARTS) // PARTS)

        return carry

    lax.fori_loop(0, NSHIP, forward, 0)

    def row_pass(tiles, shifts):
        def step(i, carry):
            for h in range(2):
                rows = pl.ds(pl.multiple_of((2 * i + h) * ROWS, ROWS), ROWS)
                xs = []
                for t, b in zip(tiles, shifts):
                    for g in range(BLK // LANES):
                        x = scores[t, rows, g * LANES:(g + 1) * LANES]
                        xs.append(x if b is None else x + b[:, g * LANES:(g + 1) * LANES])
                top = tree(jnp.maximum, xs)
                lane_top[rows, :] = top
                lane_sum[rows, :] = tree(jnp.add, [jnp.exp2(x - top) for x in xs])
            return carry

        lax.fori_loop(0, BLK // (2 * ROWS), step, 0)
        for g in range(BLK // LANES):
            rows = slice(g * LANES, (g + 1) * LANES)
            tops = lane_top[rows, :]
            top = jnp.max(tops, axis=1, keepdims=True)
            total = jnp.sum(lane_sum[rows, :] * jnp.exp2(tops - top), axis=1, keepdims=True)
            part = jnp.broadcast_to(top + log2(total), (LANES, LANES))
            vec[:, g * LANES:(g + 1) * LANES] = jnp.sum(
                jnp.where(eye, part, 0.0), axis=0, keepdims=True
            )
        return vec[...]

    def to_row():
        for g in range(BLK // LANES):
            col = jnp.sum(lane_sum[g * LANES:(g + 1) * LANES, :], axis=1, keepdims=True)
            part = jnp.broadcast_to(col, (LANES, LANES))
            vec[:, g * LANES:(g + 1) * LANES] = jnp.sum(
                jnp.where(eye, part, 0.0), axis=0, keepdims=True
            )
        return vec[...]

    def plan_pass():
        def step(i, carry):
            for h in range(2):
                rows = pl.ds(pl.multiple_of((2 * i + h) * ROWS, ROWS), ROWS)
                a = bcast[rows, :]
                es = []
                for t in range(3):
                    for g in range(BLK // LANES):
                        cols = slice(g * LANES, (g + 1) * LANES)
                        e = jnp.exp2(scores[t, rows, cols] + a + (bvec[t, :, cols] - ltgt))
                        scores[t, rows, cols] = e
                        es.append(e)
                lane_sum[rows, :] = tree(jnp.add, es)
            return carry

        lax.fori_loop(0, BLK // (2 * ROWS), step, 0)
        return to_row()

    def scaled_row_sums():
        def step(i, carry):
            for h in range(2):
                rows = pl.ds(pl.multiple_of((2 * i + h) * ROWS, ROWS), ROWS)
                es = []
                for t in range(3):
                    for g in range(BLK // LANES):
                        cols = slice(g * LANES, (g + 1) * LANES)
                        es.append(scores[t, rows, cols] * qvec[t, :, cols])
                lane_sum[rows, :] = tree(jnp.add, es)
            return carry

        lax.fori_loop(0, BLK // (2 * ROWS), step, 0)
        return to_row()

    def scaled_col_sums(t):
        groups = BLK // LANES

        def step(i, sums):
            rows = pl.ds(pl.multiple_of(i * STRIP, STRIP), STRIP)
            a = bcast[rows, :]
            out = []
            for g in range(groups):
                x = scores[t, rows, g * LANES:(g + 1) * LANES] * a
                out.append(sums[g] + jnp.sum(x.reshape(STRIP // 8, 8, LANES), axis=0))
            return tuple(out)

        sums = lax.fori_loop(
            0, BLK // STRIP, step,
            tuple(jnp.zeros((8, LANES), jnp.float32) for _ in range(groups)),
        )
        return jnp.concatenate([jnp.sum(x, axis=0, keepdims=True) for x in sums], axis=1)

    def spread(v):
        for g in range(BLK // LANES):
            part = jnp.broadcast_to(v[:, g * LANES:(g + 1) * LANES], (LANES, LANES))
            col = jnp.sum(jnp.where(eye, part, 0.0), axis=1, keepdims=True)
            bcast[g * LANES:(g + 1) * LANES, :] = jnp.broadcast_to(col, (LANES, LANES))

    def col_pass(t):
        groups = BLK // LANES

        def top_step(i, tops):
            rows = pl.ds(pl.multiple_of(i * STRIP, STRIP), STRIP)
            a = bcast[rows, :]
            out = []
            for g in range(groups):
                x = scores[t, rows, g * LANES:(g + 1) * LANES] + a
                out.append(jnp.maximum(tops[g], jnp.max(x.reshape(STRIP // 8, 8, LANES), axis=0)))
            return tuple(out)

        tops = lax.fori_loop(
            0, BLK // STRIP, top_step,
            tuple(jnp.full((8, LANES), dead, jnp.float32) for _ in range(groups)),
        )
        tops = [jnp.max(x, axis=0, keepdims=True) for x in tops]

        def sum_step(i, sums):
            rows = pl.ds(pl.multiple_of(i * STRIP, STRIP), STRIP)
            a = bcast[rows, :]
            out = []
            for g in range(groups):
                x = scores[t, rows, g * LANES:(g + 1) * LANES] + a
                e = jnp.exp2(x - tops[g])
                out.append(sums[g] + jnp.sum(e.reshape(STRIP // 8, 8, LANES), axis=0))
            return tuple(out)

        sums = lax.fori_loop(
            0, BLK // STRIP, sum_step,
            tuple(jnp.zeros((8, LANES), jnp.float32) for _ in range(groups)),
        )
        return jnp.concatenate(
            [m + log2(jnp.sum(s, axis=0, keepdims=True)) for m, s in zip(tops, sums)], axis=1
        )

    def row_round(it, mine):
        row_box[it, 0] = mine
        copies = []
        for j in range(3):
            copies.append(pltpu.make_async_remote_copy(
                src_ref=row_box.at[it, 0], dst_ref=row_box.at[it, j + 1],
                send_sem=row_s.at[it, j], recv_sem=row_r.at[it, j],
                device_id=(w, mates[j]), device_id_type=MESH,
            ))
            copies[-1].start()
        for cp in copies:
            cp.wait()
        return [row_box[it, j] for j in range(4)]

    def matches(d, block):
        b, live = extra_of(d)
        return jnp.logical_and(live, b == block)

    def merge(first, others):
        terms = [first] + [jnp.where(flag, x, dead) for flag, x in others]
        top, e = lse2(terms)
        return top + log2(functools.reduce(jnp.add, e))

    def merge_sums(first, others):
        return functools.reduce(jnp.add, [first] + [jnp.where(flag, x, 0.0) for flag, x in others])

    def col_round(it, one_pass, merge):
        for t in range(3):
            col_box[it, 0, t] = one_pass(t)
        copies = []
        for k in range(2):
            copies.append(pltpu.make_async_remote_copy(
                src_ref=col_box.at[it, 0], dst_ref=col_box.at[it, k + 1],
                send_sem=col_s.at[it, k], recv_sem=col_r.at[it, k],
                device_id=(wide_at(wide_steps[k]), c), device_id_type=MESH,
            ))
        for k in range(2):
            copies.append(pltpu.make_async_remote_copy(
                src_ref=col_box.at[it, 0, 2], dst_ref=far_box.at[it, k],
                send_sem=far_s.at[it, k], recv_sem=far_r.at[it, k],
                device_id=(wide_at(wide_steps[k + 2]), c), device_id_type=MESH,
            ))
        for cp in copies:
            cp.start()
        for cp in copies:
            cp.wait()
        before, after = col_box[it, 1, 2], col_box[it, 2, 2]
        totals = [
            merge(
                col_box[it, 0, b],
                [(matches(-1, base + b), before), (matches(1, base + b), after)],
            )
            for b in range(2)
        ]
        owner = jnp.where(
            from_before,
            jnp.where(my_pos == 0, col_box[it, 1, 0], col_box[it, 1, 1]),
            jnp.where(my_pos == 0, col_box[it, 2, 0], col_box[it, 2, 1]),
        )
        third_flag = jnp.where(
            from_before,
            jnp.where(matches(-2, my_block), 1, 0),
            jnp.where(matches(2, my_block), 1, 0),
        ) == 1
        third = jnp.where(from_before, far_box[it, 0], far_box[it, 1])
        return totals + [merge(owner, [(my_live, col_box[it, 0, 2]), (third_flag, third)])]

    own_lse[...] = row_pass([0, 1], [None, None])

    land(NCH - 1)

    extra_lse = jnp.where(my_live, row_pass([2], [None]), dead)
    top, e = lse2([own_lse[...], extra_lse])
    top, e = lse2(row_round(0, top + log2(e[0] + e[1])))
    first_lse = top + log2((e[0] + e[1]) + (e[2] + e[3]))
    spread(lsrc - first_lse)
    totals = col_round(0, col_pass, merge)
    for b in range(2):
        bvec[b] = ltgt - totals[b]
    bvec[2] = jnp.where(my_live, ltgt - totals[2], dead)

    e = row_round(1, plan_pass())
    spread(1.0 / ((e[0] + e[1]) + (e[2] + e[3])))
    totals = col_round(1, scaled_col_sums, merge_sums)
    gap = ltgt - lsrc
    for b in range(2):
        qvec[b] = 1.0 / totals[b]
        gpot_ref[b] = (epsilon * LN2) * (gap + bvec[b] - log2(totals[b]))
    qvec[2] = jnp.where(my_live, 1.0 / totals[2], 0.0)
    e = row_round(2, scaled_row_sums())
    total = (e[0] + e[1]) + (e[2] + e[3])
    fpot_ref[...] = (epsilon * LN2) * (lsrc - (first_lse + 2.0 * gap + log2(total)))
    spread(1.0 / total)

    def bary(r0):
        rows = pl.ds(pl.multiple_of(r0, PIECE), PIECE)
        level = bcast[rows, :]
        level = jnp.concatenate([level] * (BLK // LANES), axis=1)
        numer = None
        for t in range(3):
            weights = (scores[t, rows, :] * qvec[t] * level).astype(jnp.bfloat16)
            block = extra[...] if t == 2 else tgt_ref[t * BLK:(t + 1) * BLK, :]
            term = jnp.dot(weights, block, preferred_element_type=jnp.float32)
            numer = term if numer is None else numer + term
        return numer

    side = lax.rem(c, 2)
    mine0 = side * HALF
    theirs0 = HALF - mine0

    def piece_rows(p):
        return pl.ds(pl.multiple_of(p * PIECE, PIECE), PIECE)

    def part_copy(p):
        return pltpu.make_async_remote_copy(
            src_ref=part_out.at[piece_rows(p), :], dst_ref=part_in.at[piece_rows(p), :],
            send_sem=part_s.at[p], recv_sem=part_r.at[p],
            device_id=(w, mates[0]), device_id_type=MESH,
        )

    def cross_copy(p):
        return pltpu.make_async_remote_copy(
            src_ref=cross_out.at[piece_rows(p), :], dst_ref=cross_in.at[piece_rows(p), :],
            send_sem=cross_s.at[p], recv_sem=cross_r.at[p],
            device_id=(w, mates[1]), device_id_type=MESH,
        )

    def final_copy(p):
        rows = pl.ds(pl.multiple_of(mine0 + p * PIECE, PIECE), PIECE)
        return pltpu.make_async_remote_copy(
            src_ref=map_ref.at[rows, :], dst_ref=map_ref.at[rows, :],
            send_sem=fin_s.at[p], recv_sem=fin_r.at[p],
            device_id=(w, mates[0]), device_id_type=MESH,
        )

    def send_part(p, carry):
        part_out[piece_rows(p), :] = bary(theirs0 + p * PIECE).astype(jnp.bfloat16)
        part_copy(p).start()
        mine = bary(mine0 + p * PIECE)
        part_copy(p).wait()
        mine = mine + part_in[piece_rows(p), :].astype(jnp.float32)
        cross_out[piece_rows(p), :] = mine.astype(jnp.bfloat16)
        cross_copy(p).start()
        return carry

    lax.fori_loop(0, NPIECE, send_part, 0)

    def finish(p, carry):
        cross_copy(p).wait()
        both = cross_out[piece_rows(p), :].astype(jnp.float32) + cross_in[
            piece_rows(p), :
        ].astype(jnp.float32)
        rows = pl.ds(pl.multiple_of(mine0 + p * PIECE, PIECE), PIECE)
        map_ref[rows, :] = both.astype(jnp.bfloat16)
        final_copy(p).start()
        return carry

    lax.fori_loop(0, NPIECE, finish, 0)

    def drain(p, carry):
        final_copy(p).wait()
        return carry

    lax.fori_loop(0, NPIECE, drain, 0)


def shards(sources, targets, pair_target, pair_count):
    features = sources.shape[1]
    src_blocks = sources.shape[0] // BLK
    tgt_blocks = targets.shape[0] // BLK
    wide_count = lax.axis_size("wide")
    narrow_count = lax.axis_size("narrow")
    group_blocks = tgt_blocks * narrow_count
    assert ITERS == 2 and src_blocks == 1 and tgt_blocks == 2 and narrow_count == 4
    assert pair_target.shape[1] == group_blocks + narrow_count and wide_count >= 5 and wide_count % 2 == 0
    scale = LOG2E / (math.sqrt(features) * epsilon)
    lsrc = -math.log2(wide_count * src_blocks * BLK)
    ltgt = -math.log2(wide_count * narrow_count * tgt_blocks * BLK)
    consts = (scale, lsrc, ltgt, group_blocks, tgt_blocks)
    vm = pl.BlockSpec(memory_space=pltpu.VMEM)
    sm = pl.BlockSpec(memory_space=pltpu.SMEM)
    hbm = pl.BlockSpec(memory_space=pl.ANY)
    f32, bf16 = jnp.float32, jnp.bfloat16
    rounds = ITERS + 1
    dma = pltpu.SemaphoreType.DMA
    fpot, gpot, mapped = pl.pallas_call(
        functools.partial(kernel, wide_count, narrow_count, consts),
        out_shape=(
            jax.ShapeDtypeStruct((1, BLK), f32),
            jax.ShapeDtypeStruct((tgt_blocks, 1, BLK), f32),
            jax.ShapeDtypeStruct((BLK, features), bf16),
        ),
        in_specs=[sm, sm, hbm, hbm],
        out_specs=(vm, vm, vm),
        scratch_shapes=[
            pltpu.VMEM((src_blocks * BLK, features), bf16),
            pltpu.VMEM((tgt_blocks * BLK, features), bf16),
            pltpu.VMEM((3, BLK, BLK), f32),
            pltpu.VMEM((BLK, features), bf16),
            pltpu.VMEM((BLK, features), bf16),
            pltpu.VMEM((BLK, features), bf16),
            pltpu.VMEM((BLK, features), bf16),
            pltpu.VMEM((BLK, LANES), f32),
            pltpu.VMEM((BLK, LANES), f32),
            pltpu.VMEM((BLK, LANES), f32),
            pltpu.VMEM((1, BLK), f32),
            pltpu.VMEM((3, 1, BLK), f32),
            pltpu.VMEM((1, BLK), f32),
            pltpu.VMEM((rounds, 4, 1, BLK), f32),
            pltpu.VMEM((ITERS, 3, 3, 1, BLK), f32),
            pltpu.VMEM((ITERS, 2, 1, BLK), f32),
            pltpu.VMEM((3, 1, BLK), f32),
            pltpu.VMEM((HALF, features), bf16),
            pltpu.VMEM((HALF, features), bf16),
            pltpu.VMEM((HALF, features), bf16),
            pltpu.VMEM((HALF, features), bf16),
            dma((NSHIP,)), dma((NSHIP,)),
            dma((NSHIP,)), dma((NSHIP,)),
            dma((rounds, 3)), dma((rounds, 3)),
            dma((ITERS, 2)), dma((ITERS, 2)),
            dma((ITERS, 2)), dma((ITERS, 2)),
            dma((NPIECE,)), dma((NPIECE,)),
            dma((NPIECE,)), dma((NPIECE,)),
            dma((NPIECE,)), dma((NPIECE,)),
            dma((2,)),
        ],
        compiler_params=pltpu.CompilerParams(
            collective_id=0, has_side_effects=True, vmem_limit_bytes=48 * 1024 * 1024
        ),
        cost_estimate=pl.CostEstimate(
            flops=12 * BLK * BLK * features, bytes_accessed=8 * BLK * features,
            transcendentals=18 * BLK * BLK,
        ),
    )(pair_target, pair_count, sources, targets)
    return (fpot.reshape(-1), gpot.reshape(-1), mapped)


def solution(mesh):
    placed = (P("wide", None), P(("wide", "narrow"), None), P(), P())
    return jax.shard_map(
        shards,
        mesh=mesh,
        in_specs=placed,
        out_specs=(P("wide"), P(("wide", "narrow")), P("wide", None)),
        check_vma=False,
    )
```

```python
import functools
import math

import jax
import jax.numpy as jnp
from jax import lax
from jax.experimental import pallas as pl
from jax.experimental.pallas import tpu as pltpu
from jax.sharding import PartitionSpec as P

BLK = 1024
ITERS = 2
CH = 256
NCH = BLK // CH
SHIP = 64
NSHIP = BLK // SHIP
PARTS = CH // SHIP
LANES = 128
ROWS = 16
STRIP = 64
HALF = BLK // 2
PIECE = 128
NPIECE = HALF // PIECE

epsilon = 0.25
dead = -1e30
LOG2E = math.log2(math.e)
LN2 = math.log(2.0)
MESH = pl.DeviceIdType.MESH


def log2(x):
    return jnp.log(x) * LOG2E


def lse2(terms):
    top = functools.reduce(jnp.maximum, terms)
    return top, [jnp.exp2(t - top) for t in terms]


def tree(op, terms):
    while len(terms) > 1:
        pairs = [op(a, b) for a, b in zip(terms[::2], terms[1::2])]
        terms = pairs + terms[len(terms) - len(terms) % 2:]
    return terms[0]


def kernel(
    wide_count, narrow_count, consts,
    plan_ref, count_ref, src_hbm, tgt_hbm,
    fpot_ref, gpot_ref, map_ref,
    src_ref, tgt_ref, scores, relay_out, relay_in, ship, extra, bcast, lane_top, lane_sum, vec, qvec, own_lse,
    row_box, col_box, far_box, bvec, part_out, part_in, cross_out, cross_in,
    relay_s, relay_r, ship_s, ship_r, row_s, row_r, col_s, col_r, far_s, far_r,
    part_s, part_r, cross_s, cross_r, fin_s, fin_r, load_sem,
):
    scale, lsrc, ltgt, group_blocks, tgt_blocks = consts
    w = lax.axis_index("wide")
    c = lax.axis_index("narrow")

    def wide_at(d):
        return lax.rem(w + d + wide_count, wide_count)

    mates = [c + 1 - 2 * lax.rem(c, 2), c + 2 - 4 * (c // 2), 3 - c]
    wide_steps = (1, -1, 2, -2)

    load_tgt = pltpu.make_async_copy(tgt_hbm, tgt_ref, load_sem.at[0])
    load_src = pltpu.make_async_copy(src_hbm, src_ref, load_sem.at[1])
    load_tgt.start()
    load_src.start()

    barrier = pltpu.get_barrier_semaphore()
    for m in mates:
        pl.semaphore_signal(barrier, inc=1, device_id=(w, m), device_id_type=MESH)
    for d in wide_steps:
        pl.semaphore_signal(barrier, inc=1, device_id=(wide_at(d), c), device_id_type=MESH)
    pl.semaphore_wait(barrier, 7)
    load_tgt.wait()

    slot = group_blocks + c

    def extra_of(d):
        g = wide_at(d)
        block = plan_ref[g, slot]
        live = count_ref[g] > slot
        return block, live

    my_block, my_live = extra_of(0)
    my_group = my_block // group_blocks
    from_before = my_group == wide_at(-1)
    my_pos = lax.rem(my_block, tgt_blocks)
    base = w * group_blocks + c * tgt_blocks

    def as_weight(flag, shape):
        return jnp.full(shape, jnp.where(flag, 1.0, 0.0), jnp.float32).astype(jnp.bfloat16)

    def pick(flag, a, b):
        return a * as_weight(flag, a.shape) + b * as_weight(jnp.logical_not(flag), b.shape)

    even = lax.rem(w, 2) == 0
    away = jnp.where(even, wide_at(-2), wide_at(2))
    partner = jnp.where(even, w + 1, w - 1)
    user = jnp.where(even, wide_at(-1), wide_at(1))

    def chunk_rows(ch):
        return pl.ds(pl.multiple_of(ch * SHIP, SHIP), SHIP)

    def relay_copy(ch):
        return pltpu.make_async_remote_copy(
            src_ref=relay_out.at[chunk_rows(ch), :], dst_ref=relay_in.at[chunk_rows(ch), :],
            send_sem=relay_s.at[ch], recv_sem=relay_r.at[ch],
            device_id=(away, c), device_id_type=MESH,
        )

    def ship_copy(ch):
        return pltpu.make_async_remote_copy(
            src_ref=ship.at[chunk_rows(ch), :], dst_ref=extra.at[chunk_rows(ch), :],
            send_sem=ship_s.at[ch], recv_sem=ship_r.at[ch],
            device_id=(partner, c), device_id_type=MESH,
        )

    def own_chunk(first_wanted, ch):
        r0 = pl.multiple_of(ch * SHIP, SHIP)
        return pick(first_wanted, tgt_ref[pl.ds(r0, SHIP), :], tgt_ref[pl.ds(BLK + r0, SHIP), :])

    user_first = lax.rem(plan_ref[user, slot], tgt_blocks) == 0
    partner_block = plan_ref[partner, slot]
    partner_first = lax.rem(partner_block, tgt_blocks) == 0
    partner_mine = partner_block // group_blocks == w

    def relay_chunk(ch, carry):
        relay_out[chunk_rows(ch), :] = own_chunk(user_first, ch)
        relay_copy(ch).start()
        return carry

    lax.fori_loop(0, NSHIP, relay_chunk, 0)

    eye = (
        lax.broadcasted_iota(jnp.int32, (LANES, LANES), 0)
        == lax.broadcasted_iota(jnp.int32, (LANES, LANES), 1)
    )

    def dots_into(t, ch, chunk):
        cols = pl.ds(pl.multiple_of(ch * CH, CH), CH)
        scores[t, :, cols] = lax.dot_general(
            src_ref[...], chunk, (((1,), (1,)), ((), ())), preferred_element_type=jnp.float32
        ) * scale

    def own_dots(i):
        r0 = pl.multiple_of(i * CH, CH)
        dots_into(i // NCH, lax.rem(i, NCH), tgt_ref[pl.ds(r0, CH), :])

    def land(i):
        for p in range(PARTS):
            ship_copy(PARTS * i + p).wait()
        dots_into(2, i, extra[pl.ds(pl.multiple_of(i * CH, CH), CH), :])

    load_src.wait()

    def forward(ch, carry):
        @pl.when(lax.rem(ch, 2) == 0)
        def _():
            own_dots(ch // 2)

        relay_copy(ch).wait()
        ship[chunk_rows(ch), :] = pick(
            partner_mine, own_chunk(partner_first, ch), relay_in[chunk_rows(ch), :]
        )
        ship_copy(ch).start()

        @pl.when(jnp.logical_and(lax.rem(ch, PARTS) == 1, ch > PARTS))
        def _():
            land((ch - PARTS) // PARTS)

        return carry

    lax.fori_loop(0, NSHIP, forward, 0)

    def row_pass(tiles, shifts):
        def step(i, carry):
            for h in range(2):
                rows = pl.ds(pl.multiple_of((2 * i + h) * ROWS, ROWS), ROWS)
                xs = []
                for t, b in zip(tiles, shifts):
                    for g in range(BLK // LANES):
                        x = scores[t, rows, g * LANES:(g + 1) * LANES]
                        xs.append(x if b is None else x + b[:, g * LANES:(g + 1) * LANES])
                top = tree(jnp.maximum, xs)
                lane_top[rows, :] = top
                lane_sum[rows, :] = tree(jnp.add, [jnp.exp2(x - top) for x in xs])
            return carry

        lax.fori_loop(0, BLK // (2 * ROWS), step, 0)
        for g in range(BLK // LANES):
            rows = slice(g * LANES, (g + 1) * LANES)
            tops = lane_top[rows, :]
            top = jnp.max(tops, axis=1, keepdims=True)
            total = jnp.sum(lane_sum[rows, :] * jnp.exp2(tops - top), axis=1, keepdims=True)
            part = jnp.broadcast_to(top + log2(total), (LANES, LANES))
            vec[:, g * LANES:(g + 1) * LANES] = jnp.sum(
                jnp.where(eye, part, 0.0), axis=0, keepdims=True
            )
        return vec[...]

    def to_row():
        for g in range(BLK // LANES):
            col = jnp.sum(lane_sum[g * LANES:(g + 1) * LANES, :], axis=1, keepdims=True)
            part = jnp.broadcast_to(col, (LANES, LANES))
            vec[:, g * LANES:(g + 1) * LANES] = jnp.sum(
                jnp.where(eye, part, 0.0), axis=0, keepdims=True
            )
        return vec[...]

    def plan_pass():
        def step(i, carry):
            for h in range(2):
                rows = pl.ds(pl.multiple_of((2 * i + h) * ROWS, ROWS), ROWS)
                a = bcast[rows, :]
                es = []
                for t in range(3):
                    for g in range(BLK // LANES):
                        cols = slice(g * LANES, (g + 1) * LANES)
                        e = jnp.exp2(scores[t, rows, cols] + a + (bvec[t, :, cols] - ltgt))
                        scores[t, rows, cols] = e
                        es.append(e)
                lane_sum[rows, :] = tree(jnp.add, es)
            return carry

        lax.fori_loop(0, BLK // (2 * ROWS), step, 0)
        return to_row()

    def scaled_row_sums():
        def step(i, carry):
            for h in range(2):
                rows = pl.ds(pl.multiple_of((2 * i + h) * ROWS, ROWS), ROWS)
                es = []
                for t in range(3):
                    for g in range(BLK // LANES):
                        cols = slice(g * LANES, (g + 1) * LANES)
                        es.append(scores[t, rows, cols] * qvec[t, :, cols])
                lane_sum[rows, :] = tree(jnp.add, es)
            return carry

        lax.fori_loop(0, BLK // (2 * ROWS), step, 0)
        return to_row()

    def scaled_col_sums(t):
        groups = BLK // LANES

        def step(i, sums):
            rows = pl.ds(pl.multiple_of(i * STRIP, STRIP), STRIP)
            a = bcast[rows, :]
            out = []
            for g in range(groups):
                x = scores[t, rows, g * LANES:(g + 1) * LANES] * a
                out.append(sums[g] + jnp.sum(x.reshape(STRIP // 8, 8, LANES), axis=0))
            return tuple(out)

        sums = lax.fori_loop(
            0, BLK // STRIP, step,
            tuple(jnp.zeros((8, LANES), jnp.float32) for _ in range(groups)),
        )
        return jnp.concatenate([jnp.sum(x, axis=0, keepdims=True) for x in sums], axis=1)

    def spread(v):
        for g in range(BLK // LANES):
            part = jnp.broadcast_to(v[:, g * LANES:(g + 1) * LANES], (LANES, LANES))
            col = jnp.sum(jnp.where(eye, part, 0.0), axis=1, keepdims=True)
            bcast[g * LANES:(g + 1) * LANES, :] = jnp.broadcast_to(col, (LANES, LANES))

    def col_pass(t):
        groups = BLK // LANES

        def top_step(i, tops):
            rows = pl.ds(pl.multiple_of(i * STRIP, STRIP), STRIP)
            a = bcast[rows, :]
            out = []
            for g in range(groups):
                x = scores[t, rows, g * LANES:(g + 1) * LANES] + a
                out.append(jnp.maximum(tops[g], jnp.max(x.reshape(STRIP // 8, 8, LANES), axis=0)))
            return tuple(out)

        tops = lax.fori_loop(
            0, BLK // STRIP, top_step,
            tuple(jnp.full((8, LANES), dead, jnp.float32) for _ in range(groups)),
        )
        tops = [jnp.max(x, axis=0, keepdims=True) for x in tops]

        def sum_step(i, sums):
            rows = pl.ds(pl.multiple_of(i * STRIP, STRIP), STRIP)
            a = bcast[rows, :]
            out = []
            for g in range(groups):
                x = scores[t, rows, g * LANES:(g + 1) * LANES] + a
                e = jnp.exp2(x - tops[g])
                out.append(sums[g] + jnp.sum(e.reshape(STRIP // 8, 8, LANES), axis=0))
            return tuple(out)

        sums = lax.fori_loop(
            0, BLK // STRIP, sum_step,
            tuple(jnp.zeros((8, LANES), jnp.float32) for _ in range(groups)),
        )
        return jnp.concatenate(
            [m + log2(jnp.sum(s, axis=0, keepdims=True)) for m, s in zip(tops, sums)], axis=1
        )

    def row_round(it, mine):
        row_box[it, 0] = mine
        copies = []
        for j in range(3):
            copies.append(pltpu.make_async_remote_copy(
                src_ref=row_box.at[it, 0], dst_ref=row_box.at[it, j + 1],
                send_sem=row_s.at[it, j], recv_sem=row_r.at[it, j],
                device_id=(w, mates[j]), device_id_type=MESH,
            ))
            copies[-1].start()
        for cp in copies:
            cp.wait()
        return [row_box[it, j] for j in range(4)]

    def matches(d, block):
        b, live = extra_of(d)
        return jnp.logical_and(live, b == block)

    def merge(first, others):
        terms = [first] + [jnp.where(flag, x, dead) for flag, x in others]
        top, e = lse2(terms)
        return top + log2(functools.reduce(jnp.add, e))

    def merge_sums(first, others):
        return functools.reduce(jnp.add, [first] + [jnp.where(flag, x, 0.0) for flag, x in others])

    def col_round(it, one_pass, merge):
        for t in range(3):
            col_box[it, 0, t] = one_pass(t)
        copies = []
        for k in range(2):
            copies.append(pltpu.make_async_remote_copy(
                src_ref=col_box.at[it, 0], dst_ref=col_box.at[it, k + 1],
                send_sem=col_s.at[it, k], recv_sem=col_r.at[it, k],
                device_id=(wide_at(wide_steps[k]), c), device_id_type=MESH,
            ))
        for k in range(2):
            copies.append(pltpu.make_async_remote_copy(
                src_ref=col_box.at[it, 0, 2], dst_ref=far_box.at[it, k],
                send_sem=far_s.at[it, k], recv_sem=far_r.at[it, k],
                device_id=(wide_at(wide_steps[k + 2]), c), device_id_type=MESH,
            ))
        for cp in copies:
            cp.start()
        for cp in copies:
            cp.wait()
        before, after = col_box[it, 1, 2], col_box[it, 2, 2]
        totals = [
            merge(
                col_box[it, 0, b],
                [(matches(-1, base + b), before), (matches(1, base + b), after)],
            )
            for b in range(2)
        ]
        owner = jnp.where(
            from_before,
            jnp.where(my_pos == 0, col_box[it, 1, 0], col_box[it, 1, 1]),
            jnp.where(my_pos == 0, col_box[it, 2, 0], col_box[it, 2, 1]),
        )
        third_flag = jnp.where(
            from_before,
            jnp.where(matches(-2, my_block), 1, 0),
            jnp.where(matches(2, my_block), 1, 0),
        ) == 1
        third = jnp.where(from_before, far_box[it, 0], far_box[it, 1])
        return totals + [merge(owner, [(my_live, col_box[it, 0, 2]), (third_flag, third)])]

    own_lse[...] = row_pass([0, 1], [None, None])

    land(NCH - 1)

    extra_lse = jnp.where(my_live, row_pass([2], [None]), dead)
    top, e = lse2([own_lse[...], extra_lse])
    top, e = lse2(row_round(0, top + log2(e[0] + e[1])))
    first_lse = top + log2((e[0] + e[1]) + (e[2] + e[3]))
    spread(lsrc - first_lse)
    totals = col_round(0, col_pass, merge)
    for b in range(2):
        bvec[b] = ltgt - totals[b]
    bvec[2] = jnp.where(my_live, ltgt - totals[2], dead)

    e = row_round(1, plan_pass())
    spread(1.0 / ((e[0] + e[1]) + (e[2] + e[3])))
    totals = col_round(1, scaled_col_sums, merge_sums)
    gap = ltgt - lsrc
    for b in range(2):
        qvec[b] = 1.0 / totals[b]
        gpot_ref[b] = (epsilon * LN2) * (gap + bvec[b] - log2(totals[b]))
    qvec[2] = jnp.where(my_live, 1.0 / totals[2], 0.0)

    def bary(r0):
        rows = pl.ds(pl.multiple_of(r0, PIECE), PIECE)
        numer = None
        for t in range(3):
            weights = (scores[t, rows, :] * qvec[t]).astype(jnp.bfloat16)
            block = extra[...] if t == 2 else tgt_ref[t * BLK:(t + 1) * BLK, :]
            term = jnp.dot(weights, block, preferred_element_type=jnp.float32)
            numer = term if numer is None else numer + term
        return numer

    side = lax.rem(c, 2)
    mine0 = side * HALF
    theirs0 = HALF - mine0

    def piece_rows(p):
        return pl.ds(pl.multiple_of(p * PIECE, PIECE), PIECE)

    def part_copy(p):
        return pltpu.make_async_remote_copy(
            src_ref=part_out.at[piece_rows(p), :], dst_ref=part_in.at[piece_rows(p), :],
            send_sem=part_s.at[p], recv_sem=part_r.at[p],
            device_id=(w, mates[0]), device_id_type=MESH,
        )

    def cross_copy(p):
        return pltpu.make_async_remote_copy(
            src_ref=cross_out.at[piece_rows(p), :], dst_ref=cross_in.at[piece_rows(p), :],
            send_sem=cross_s.at[p], recv_sem=cross_r.at[p],
            device_id=(w, mates[1]), device_id_type=MESH,
        )

    def final_copy(p):
        rows = pl.ds(pl.multiple_of(mine0 + p * PIECE, PIECE), PIECE)
        return pltpu.make_async_remote_copy(
            src_ref=map_ref.at[rows, :], dst_ref=map_ref.at[rows, :],
            send_sem=fin_s.at[p], recv_sem=fin_r.at[p],
            device_id=(w, mates[0]), device_id_type=MESH,
        )

    def send_part(p, carry):
        part_out[piece_rows(p), :] = bary(theirs0 + p * PIECE).astype(jnp.bfloat16)
        part_copy(p).start()
        mine = bary(mine0 + p * PIECE)
        part_copy(p).wait()
        mine = mine + part_in[piece_rows(p), :].astype(jnp.float32)
        cross_out[piece_rows(p), :] = mine.astype(jnp.bfloat16)
        cross_copy(p).start()
        return carry

    lax.fori_loop(0, NPIECE, send_part, 0)

    e = row_round(2, scaled_row_sums())
    total = (e[0] + e[1]) + (e[2] + e[3])
    fpot_ref[...] = (epsilon * LN2) * (lsrc - (first_lse + 2.0 * gap + log2(total)))
    spread(1.0 / total)

    def finish(p, carry):
        cross_copy(p).wait()
        both = cross_out[piece_rows(p), :].astype(jnp.float32) + cross_in[
            piece_rows(p), :
        ].astype(jnp.float32)
        rows = pl.ds(pl.multiple_of(mine0 + p * PIECE, PIECE), PIECE)
        level = jnp.concatenate([bcast[rows, :]] * (both.shape[1] // LANES), axis=1)
        map_ref[rows, :] = (both * level).astype(jnp.bfloat16)
        final_copy(p).start()
        return carry

    lax.fori_loop(0, NPIECE, finish, 0)

    def drain(p, carry):
        final_copy(p).wait()
        return carry

    lax.fori_loop(0, NPIECE, drain, 0)


def shards(sources, targets, pair_target, pair_count):
    features = sources.shape[1]
    src_blocks = sources.shape[0] // BLK
    tgt_blocks = targets.shape[0] // BLK
    wide_count = lax.axis_size("wide")
    narrow_count = lax.axis_size("narrow")
    group_blocks = tgt_blocks * narrow_count
    assert ITERS == 2 and src_blocks == 1 and tgt_blocks == 2 and narrow_count == 4
    assert pair_target.shape[1] == group_blocks + narrow_count and wide_count >= 5 and wide_count % 2 == 0
    scale = LOG2E / (math.sqrt(features) * epsilon)
    lsrc = -math.log2(wide_count * src_blocks * BLK)
    ltgt = -math.log2(wide_count * narrow_count * tgt_blocks * BLK)
    consts = (scale, lsrc, ltgt, group_blocks, tgt_blocks)
    vm = pl.BlockSpec(memory_space=pltpu.VMEM)
    sm = pl.BlockSpec(memory_space=pltpu.SMEM)
    hbm = pl.BlockSpec(memory_space=pl.ANY)
    f32, bf16 = jnp.float32, jnp.bfloat16
    rounds = ITERS + 1
    dma = pltpu.SemaphoreType.DMA
    fpot, gpot, mapped = pl.pallas_call(
        functools.partial(kernel, wide_count, narrow_count, consts),
        out_shape=(
            jax.ShapeDtypeStruct((1, BLK), f32),
            jax.ShapeDtypeStruct((tgt_blocks, 1, BLK), f32),
            jax.ShapeDtypeStruct((BLK, features), bf16),
        ),
        in_specs=[sm, sm, hbm, hbm],
        out_specs=(vm, vm, vm),
        scratch_shapes=[
            pltpu.VMEM((src_blocks * BLK, features), bf16),
            pltpu.VMEM((tgt_blocks * BLK, features), bf16),
            pltpu.VMEM((3, BLK, BLK), f32),
            pltpu.VMEM((BLK, features), bf16),
            pltpu.VMEM((BLK, features), bf16),
            pltpu.VMEM((BLK, features), bf16),
            pltpu.VMEM((BLK, features), bf16),
            pltpu.VMEM((BLK, LANES), f32),
            pltpu.VMEM((BLK, LANES), f32),
            pltpu.VMEM((BLK, LANES), f32),
            pltpu.VMEM((1, BLK), f32),
            pltpu.VMEM((3, 1, BLK), f32),
            pltpu.VMEM((1, BLK), f32),
            pltpu.VMEM((rounds, 4, 1, BLK), f32),
            pltpu.VMEM((ITERS, 3, 3, 1, BLK), f32),
            pltpu.VMEM((ITERS, 2, 1, BLK), f32),
            pltpu.VMEM((3, 1, BLK), f32),
            pltpu.VMEM((HALF, features), bf16),
            pltpu.VMEM((HALF, features), bf16),
            pltpu.VMEM((HALF, features), bf16),
            pltpu.VMEM((HALF, features), bf16),
            dma((NSHIP,)), dma((NSHIP,)),
            dma((NSHIP,)), dma((NSHIP,)),
            dma((rounds, 3)), dma((rounds, 3)),
            dma((ITERS, 2)), dma((ITERS, 2)),
            dma((ITERS, 2)), dma((ITERS, 2)),
            dma((NPIECE,)), dma((NPIECE,)),
            dma((NPIECE,)), dma((NPIECE,)),
            dma((NPIECE,)), dma((NPIECE,)),
            dma((2,)),
        ],
        compiler_params=pltpu.CompilerParams(
            collective_id=0, has_side_effects=True, vmem_limit_bytes=48 * 1024 * 1024
        ),
        cost_estimate=pl.CostEstimate(
            flops=12 * BLK * BLK * features, bytes_accessed=8 * BLK * features,
            transcendentals=18 * BLK * BLK,
        ),
    )(pair_target, pair_count, sources, targets)
    return (fpot.reshape(-1), gpot.reshape(-1), mapped)


def solution(mesh):
    placed = (P("wide", None), P(("wide", "narrow"), None), P(), P())
    return jax.shard_map(
        shards,
        mesh=mesh,
        in_specs=placed,
        out_specs=(P("wide"), P(("wide", "narrow")), P("wide", None)),
        check_vma=False,
    )
```
